32 devices in a mesh: grp: 2 (over x), row: 16 (over z, y, core).
Axes of the slice: x: 2, y: 2, z: 4, core: 2. Of those that a mesh axis runs over, the one named last changes fastest.
Arguments:
- amplitudes: bfloat16 [12288, 6144], P(('grp', 'row')), parts along dimension 0, may hold values from -6 to 6
- integrals: bfloat16 [12288, 6144], P(('grp', 'row')), parts along dimension 0, may hold values from -0.078125 to 0.078125
- occupied_energy: float32 [96], replicated, may hold values from 0.3 to 3
- virtual_energy: float32 [8, 64], replicated, may hold values from 0.05 to 4
- pair_irrep: int32 [192], P('grp'), parts along dimension 0, may hold values from 0 to 7
Outputs:
- increment: bfloat16 [12288, 6144], P(('grp', 'row')), parts along dimension 0
The draws below stay inside these ranges and needn't reach their ends.
There are 2 independent parts, one for each index of `grp`. The reference program is written for one: setup_inputs(seed, part) draws one part's arguments, and reference() takes and returns one part's arrays. A program takes and returns all parts, laid end to end along the dimension named above; an argument that names none is the same for every part. Nothing has to cross between parts.
All inputs are finite; a program needn't handle non-finite values.
Results may differ from the reference program's by a relative error of at most 0.001.
Values may be sent and summed in bfloat16 or wider, within the bound.
A program may use at most 192 MiB of HBM per device.

```python
import math
import jax
import jax.numpy as jnp

OCC = 96
VIRT_IRREP = 64
IRREPS = 8
PAIRS = 6144


def set_ends(values, rng, low, high):
    dims = values.shape
    index_at = [jax.random.randint(jax.random.fold_in(rng, axis), (), 0, dims[axis]) for axis in range(len(dims))]
    values = values.at[tuple(index_at)].set(low)
    longest = dims.index(max(dims))
    index_at[longest] = (index_at[longest] + 1) % dims[longest]
    return values.at[tuple(index_at)].set(high)


def block_scale(key, dims, split, smallest, high):
    level, own = 1.0, jax.random.fold_in(key, 6)
    for axis_at, blocks in split:
        draws = jnp.exp(jax.random.uniform(jax.random.fold_in(own, axis_at), (blocks,), jnp.float32, smallest / len(split), high / len(split)))
        level = level * jnp.repeat(draws, dims[axis_at] // blocks).reshape([-1 if axis == axis_at else 1 for axis in range(len(dims))])
    return level


def noise(rng, shape, deviation, most, split=(), held_as=jnp.bfloat16):
    drawn = deviation * jax.random.normal(rng, shape, jnp.float32)
    if split:
        drawn = drawn * block_scale(rng, shape, split, -0.22, 0.18)
    return jnp.clip(drawn, -most, most).astype(held_as)


def setup_inputs(seed: int = 0, part: int = 0) -> dict:
    streams_of = jax.random.split(jax.random.key(seed), 6)
    part_splits = jax.random.split(jax.random.fold_in(streams_of[5], part), 6)
    amplitudes = noise(part_splits[0], (PAIRS, PAIRS), 1.0, 6.0, ((0, 16),))
    integrals = noise(part_splits[1], (PAIRS, PAIRS), PAIRS ** -0.5, 0.078125, ((0, 16),))
    occupied_energy = jnp.clip(jnp.exp(jax.random.uniform(streams_of[2], (OCC,), jnp.float32, math.log(0.3), math.log(3.0))), 0.3, 3.0)
    virtual_energy = jnp.clip(jnp.exp(jax.random.uniform(streams_of[3], (IRREPS, VIRT_IRREP), jnp.float32, math.log(0.05), math.log(4.0))), 0.05, 4.0)
    pair_irrep = set_ends(jax.random.randint(part_splits[4], (OCC,), 0, IRREPS), jax.random.fold_in(part_splits[4], 1), 0, IRREPS - 1).astype(jnp.int32)
    return dict(amplitudes=amplitudes, integrals=integrals, occupied_energy=occupied_energy, virtual_energy=virtual_energy, pair_irrep=pair_irrep)


def pair_energies(occupied_energy, virtual_energy, pair_irrep):
    onehot = (pair_irrep[:, None] == jnp.arange(IRREPS)[None, :]).astype(jnp.float32)
    virtual = jnp.sum(onehot[:, :, None] * virtual_energy[None, :, :], axis=1)
    return (virtual + occupied_energy[:, None]).reshape(-1)


def reference(amplitudes, integrals, occupied_energy, virtual_energy, pair_irrep):
    pair_energy = pair_energies(occupied_energy, virtual_energy, pair_irrep)
    cycle_term = jnp.dot(amplitudes, integrals, preferred_element_type=jnp.float32)
    denominator = pair_energy[:, None] + pair_energy[None, :]
    return (cycle_term / denominator).astype(jnp.bfloat16)
```

```python
import functools
import jax
import jax.numpy as jnp
from jax import lax
from jax.experimental import pallas as pl
from jax.experimental.pallas import tpu as pltpu
from jax.sharding import PartitionSpec as P

QUAD = 4
MESH = pl.DeviceIdType.MESH


def pair_energies(occupied_energy, virtual_energy, pair_irrep):
    labels = jnp.arange(virtual_energy.shape[0])
    onehot = (pair_irrep[:, None] == labels[None, :]).astype(jnp.float32)
    virtual = jnp.sum(onehot[:, :, None] * virtual_energy[None, :, :], axis=1)
    return (virtual + occupied_energy[:, None]).reshape(-1)


def kernel(layers, chunks, a_ref, b_ref, row_ref, col_ref, out_ref, a_all, b_all, c_all,
           local_sem, bq_send, bq_recv, a_send, a_recv, z_send, z_recv, c_send, c_recv, c_local):
    rows = a_ref.shape[0]
    width = b_all.shape[2]
    quarter = chunks * width
    layer_rows = QUAD * rows
    me = lax.axis_index("row")
    layer, spot = me // QUAD, me % QUAD
    half, core = spot // 2, spot % 2
    spots = ((half * 2) + (1 - core), (1 - half) * 2 + core, (1 - half) * 2 + (1 - core))
    peers = [layer * QUAD + s for s in spots]
    first = layer * QUAD
    has_below, has_above = layer > 0, layer < layers - 1

    def local_a():
        return pltpu.make_async_copy(a_ref, a_all.at[spot], local_sem.at[0])

    def cols(owner, c):
        return pl.ds(pl.multiple_of(owner * quarter + c * width, width), width)

    def local_b(c):
        return pltpu.make_async_copy(
            b_ref.at[:, cols(spot, c)], b_all.at[c, pl.ds(me * rows, rows), :], local_sem.at[1 + c])

    def quad_b(c, p):
        return pltpu.make_async_remote_copy(
            src_ref=b_ref.at[:, cols(spots[p], c)], dst_ref=b_all.at[c, pl.ds(me * rows, rows), :],
            send_sem=bq_send.at[c, p], recv_sem=bq_recv.at[c, p],
            device_id={"row": peers[p]}, device_id_type=MESH)

    def quad_a(p):
        if p == 2:
            return pltpu.make_async_remote_copy(
                src_ref=a_all.at[spots[1]], dst_ref=a_all.at[spots[1]],
                send_sem=a_send.at[p], recv_sem=a_recv.at[p],
                device_id={"row": peers[0]}, device_id_type=MESH)
        return pltpu.make_async_remote_copy(
            src_ref=a_ref, dst_ref=a_all.at[spot],
            send_sem=a_send.at[p], recv_sem=a_recv.at[p],
            device_id={"row": peers[p]}, device_id_type=MESH)

    def along(c, owner, up):
        block = b_all.at[c, pl.ds(owner * layer_rows, layer_rows), :]
        return pltpu.make_async_remote_copy(
            src_ref=block, dst_ref=block,
            send_sem=z_send.at[up, c, owner], recv_sem=z_recv.at[c, owner],
            device_id={"row": me + QUAD if up else me - QUAD}, device_id_type=MESH)

    def result(c, p):
        return pltpu.make_async_remote_copy(
            src_ref=c_all.at[c, pl.ds(spots[p] * rows, rows), :], dst_ref=out_ref.at[:, cols(spot, c)],
            send_sem=c_send.at[c, p], recv_sem=c_recv.at[c, p],
            device_id={"row": peers[p]}, device_id_type=MESH)

    def local_result(c):
        return pltpu.make_async_copy(
            c_all.at[c, pl.ds(spot * rows, rows), :], out_ref.at[:, cols(spot, c)], c_local.at[c])

    barrier = pltpu.get_barrier_semaphore()
    for p in range(3):
        pl.semaphore_signal(barrier, inc=1, device_id={"row": peers[p]}, device_id_type=MESH)

    @pl.when(has_below)
    def _():
        pl.semaphore_signal(barrier, inc=1, device_id={"row": me - QUAD}, device_id_type=MESH)

    @pl.when(has_above)
    def _():
        pl.semaphore_signal(barrier, inc=1, device_id={"row": me + QUAD}, device_id_type=MESH)

    pl.semaphore_wait(barrier, 3 + has_below.astype(jnp.int32) + has_above.astype(jnp.int32))

    @pl.loop(0, chunks)
    def _(c):
        local_b(c).start()
        for p in range(3):
            quad_b(c, p).start()

    local_a().start()
    quad_a(0).start()

    @pl.loop(0, chunks)
    def _(c):
        local_b(c).wait()
        for p in range(3):
            quad_b(c, p).wait_recv()

        @pl.when(has_above)
        def _():
            along(c, layer, 1).start()

        @pl.when(has_below)
        def _():
            along(c, layer, 0).start()

    quad_a(1).start()

    def forward(c):
        for d in range(1, layers - 1):
            @pl.when((layer >= d) & has_above)
            def _():
                along(c, layer - d, 1).wait_recv()
                along(c, layer - d, 1).start()

            @pl.when((layer + d < layers) & has_below)
            def _():
                along(c, layer + d, 0).wait_recv()
                along(c, layer + d, 0).start()

    def compute(c):
        @pl.loop(0, layers)
        def _(owner):
            from_below, from_above = owner < layer, owner > layer
            passed_on = (from_below & has_above) | (from_above & has_below)

            @pl.when((from_below | from_above) & jnp.logical_not(passed_on))
            def _():
                along(c, owner, 0).wait_recv()

        @pl.loop(0, QUAD)
        def _(s):
            total = jnp.dot(a_all[s], b_all[c], preferred_element_type=jnp.float32)
            denominator = row_ref[s] + col_ref[c]
            at = pl.ds(pl.multiple_of(s * rows, rows), rows)
            c_all[c, at, :] = (total / denominator).astype(jnp.bfloat16)

        for p in (1, 2, 0):
            result(c, p).start()
        local_result(c).start()

    lag = 2

    @pl.loop(0, lag)
    def _(c):
        forward(c)

    local_a().wait()
    quad_a(1).wait_recv()
    quad_a(2).start()
    quad_a(0).wait_recv()
    quad_a(2).wait_recv()

    @pl.loop(lag, chunks + lag)
    def _(c):
        @pl.when(c < chunks)
        def _():
            forward(c)
        compute(c - lag)

    for p in range(3):
        quad_a(p).wait_send()

    @pl.loop(0, chunks)
    def _(c):
        local_result(c).wait()
        for p in range(3):
            quad_b(c, p).wait_send()
            result(c, p).wait()

        @pl.loop(0, layers)
        def _(owner):
            @pl.when((owner <= layer) & has_above)
            def _():
                along(c, owner, 1).wait_send()

            @pl.when((owner >= layer) & has_below)
            def _():
                along(c, owner, 0).wait_send()


def shards(amplitudes, integrals, occupied_energy, virtual_energy, pair_irrep):
    devices = lax.axis_size("row")
    layers = devices // QUAD
    rows, columns = amplitudes.shape
    depth = integrals.shape[0] * devices
    quarter = columns // QUAD
    width = 256
    chunks = quarter // width
    position = lax.axis_index("row")
    pair_energy = pair_energies(occupied_energy, virtual_energy, pair_irrep)
    row_energy = lax.dynamic_slice_in_dim(pair_energy, position // QUAD * QUAD * rows, QUAD * rows)
    col_energy = lax.dynamic_slice_in_dim(pair_energy, position % QUAD * quarter, quarter)
    dma = pltpu.SemaphoreType.DMA
    return pl.pallas_call(
        functools.partial(kernel, layers, chunks),
        out_shape=jax.ShapeDtypeStruct((rows, columns), jnp.bfloat16),
        in_specs=[pl.BlockSpec(memory_space=pl.ANY)] * 2 + [pl.BlockSpec(memory_space=pltpu.VMEM)] * 2,
        out_specs=pl.BlockSpec(memory_space=pl.ANY),
        scratch_shapes=[
            pltpu.VMEM((QUAD, rows, depth), jnp.bfloat16),
            pltpu.VMEM((chunks, depth, width), jnp.bfloat16),
            pltpu.VMEM((chunks, QUAD * rows, width), jnp.bfloat16),
            dma((1 + chunks,)),
            dma((chunks, 3)),
            dma((chunks, 3)),
            dma((3,)),
            dma((3,)),
            dma((2, chunks, layers)),
            dma((chunks, layers)),
            dma((chunks, 3)),
            dma((chunks, 3)),
            dma((chunks,)),
        ],
        compiler_params=pltpu.CompilerParams(
            collective_id=0, has_side_effects=True, vmem_limit_bytes=58 * 1024 * 1024),
        cost_estimate=pl.CostEstimate(
            flops=2 * rows * depth * columns, bytes_accessed=6 * rows * columns, transcendentals=0),
    )(amplitudes, integrals, row_energy.reshape(QUAD, rows, 1), col_energy.reshape(chunks, 1, width))


def solution(mesh):
    in_specs = (P(("grp", "row"), None), P(("grp", "row"), None), P(), P(), P("grp"))
    out_specs = P(("grp", "row"), None)
    return jax.shard_map(shards, mesh=mesh, in_specs=in_specs, out_specs=out_specs, check_vma=False)
```

```python
import functools
import jax
import jax.numpy as jnp
from jax import lax
from jax.experimental import pallas as pl
from jax.experimental.pallas import tpu as pltpu
from jax.sharding import PartitionSpec as P

QUAD = 4
MESH = pl.DeviceIdType.MESH


def pair_energies(occupied_energy, virtual_energy, pair_irrep):
    labels = jnp.arange(virtual_energy.shape[0])
    onehot = (pair_irrep[:, None] == labels[None, :]).astype(jnp.float32)
    virtual = jnp.sum(onehot[:, :, None] * virtual_energy[None, :, :], axis=1)
    return (virtual + occupied_energy[:, None]).reshape(-1)


def kernel(layers, chunks, shed, a_ref, b_ref, row_ref, col_ref, out_ref, a_all, b_all, c_all,
           a_shed, c_shed, local_sem, bq_send, bq_recv, a_send, a_recv, z_send, z_recv, c_send, c_recv,
           c_local, az_send, az_recv, as_send, as_recv, cz_send, cz_recv, d_send, d_recv, d_local):
    rows = a_ref.shape[0]
    part = rows // 2
    width = b_all.shape[2]
    quarter = chunks * width
    layer_rows = QUAD * rows
    me = lax.axis_index("row")
    layer, spot = me // QUAD, me % QUAD
    half, core = spot // 2, spot % 2
    spots = ((half * 2) + (1 - core), (1 - half) * 2 + core, (1 - half) * 2 + (1 - core))
    peers = [layer * QUAD + s for s in spots]
    has_below, has_above = layer > 0, layer < layers - 1
    is_end = (layer == 0) | (layer == layers - 1)
    is_helper = (layer == 1) | (layer == layers - 2)
    upper = layer * 2 // layers
    depth = layer + upper * (layers - 1 - 2 * layer)
    mate = me + QUAD * (1 - 2 * upper) * (1 - 2 * depth)

    def local_a():
        return pltpu.make_async_copy(a_ref, a_all.at[spot], local_sem.at[0])

    def cols(owner, c):
        return pl.ds(pl.multiple_of(owner * quarter + c * width, width), width)

    def remote(src, dst, send, recv, device):
        return pltpu.make_async_remote_copy(
            src_ref=src, dst_ref=dst, send_sem=send, recv_sem=recv,
            device_id={"row": device}, device_id_type=MESH)

    def local_b(c):
        return pltpu.make_async_copy(
            b_ref.at[:, cols(spot, c)], b_all.at[c, pl.ds(me * rows, rows), :], local_sem.at[1 + c])

    def quad_b(c, p):
        return remote(b_ref.at[:, cols(spots[p], c)], b_all.at[c, pl.ds(me * rows, rows), :],
                      bq_send.at[c, p], bq_recv.at[c, p], peers[p])

    def quad_a(p):
        if p == 2:
            return remote(a_all.at[spots[1]], a_all.at[spots[1]], a_send.at[p], a_recv.at[p], peers[0])
        return remote(a_ref, a_all.at[spot], a_send.at[p], a_recv.at[p], peers[p])

    def along(c, owner, up):
        block = b_all.at[c, pl.ds(owner * layer_rows, layer_rows), :]
        return remote(block, block, z_send.at[up, c, owner], z_recv.at[c, owner],
                      me + QUAD if up else me - QUAD)

    def result(c, p):
        return remote(c_all.at[c, pl.ds(spots[p] * rows, rows), :], out_ref.at[:, cols(spot, c)],
                      c_send.at[c, p], c_recv.at[c, p], peers[p])

    def local_result(c):
        return pltpu.make_async_copy(
            c_all.at[c, pl.ds(spot * rows, rows), :], out_ref.at[:, cols(spot, c)], c_local.at[c])

    def piece(u):
        return pl.ds(u * part, part)

    def shed_z(k):
        u = 1 if k == 0 else 0
        src = a_all.at[spots[1], piece(u), :] if k == 2 else a_ref.at[piece(u), :]
        return remote(src, a_shed.at[spots[1] if k == 2 else spot, piece(u), :],
                      az_send.at[k], az_recv.at[k], mate)

    def shed_quad(k):
        at = a_shed.at[spot if k < 3 else spots[1], piece((1, 1, 0, 1, 0)[k]), :]
        return remote(at, at, as_send.at[k], as_recv.at[k], peers[1] if k == 0 else peers[0])

    order = ((3, 1), (0, 1), (3, 0), (0, 0), (1, 1), (2, 1), (1, 0), (2, 0))

    def spot_of(p):
        return spot if p == 3 else spots[p]

    def at_rows(p, u):
        return pl.ds(spot_of(p) * rows + u * part, part)

    def back(o, h):
        at = at_rows(*order[h])
        return remote(c_shed.at[o, at, :], c_all.at[o, at, :], cz_send.at[o, h], cz_recv.at[o, h], mate)

    def deal(o, h):
        p, u = order[h]
        src, dst = c_all.at[o, at_rows(p, u), :], out_ref.at[piece(u), cols(spot, o)]
        if p == 3:
            return pltpu.make_async_copy(src, dst, d_local.at[o, u])
        return remote(src, dst, d_send.at[o, u, p], d_recv.at[o, u, p], peers[p])

    barrier = pltpu.get_barrier_semaphore()
    for p in range(3):
        pl.semaphore_signal(barrier, inc=1, device_id={"row": peers[p]}, device_id_type=MESH)

    @pl.when(has_below)
    def _():
        pl.semaphore_signal(barrier, inc=1, device_id={"row": me - QUAD}, device_id_type=MESH)

    @pl.when(has_above)
    def _():
        pl.semaphore_signal(barrier, inc=1, device_id={"row": me + QUAD}, device_id_type=MESH)

    pl.semaphore_wait(barrier, 3 + has_below.astype(jnp.int32) + has_above.astype(jnp.int32))

    @pl.loop(0, chunks)
    def _(c):
        local_b(c).start()
        for p in range(3):
            quad_b(c, p).start()

    local_a().start()
    quad_a(0).start()

    def goes_up(c):
        return has_above & ((layer < layers - 2) | (c >= shed))

    def goes_down(c):
        return has_below & ((layer > 1) | (c >= shed))

    def due(c):
        return jnp.logical_not(is_end) | (c >= shed)

    @pl.loop(0, chunks)
    def _(c):
        local_b(c).wait()
        for p in range(3):
            quad_b(c, p).wait_recv()

        @pl.when(goes_up(c))
        def _():
            along(c, layer, 1).start()

        @pl.when(goes_down(c))
        def _():
            along(c, layer, 0).start()

    quad_a(1).start()

    def forward(d, c):
        @pl.when((layer >= d) & goes_up(c))
        def _():
            along(c, layer - d, 1).wait_recv()
            along(c, layer - d, 1).start()

        @pl.when((layer + d < layers) & goes_down(c))
        def _():
            along(c, layer + d, 0).wait_recv()
            along(c, layer + d, 0).start()

    def compute(c):
        @pl.loop(0, layers)
        def _(owner):
            from_below, from_above = owner < layer, owner > layer
            passed_on = (from_below & goes_up(c)) | (from_above & goes_down(c))

            @pl.when((from_below | from_above) & jnp.logical_not(passed_on))
            def _():
                along(c, owner, 0).wait_recv()

        @pl.loop(0, QUAD)
        def _(s):
            total = jnp.dot(a_all[s], b_all[c], preferred_element_type=jnp.float32)
            denominator = row_ref[0, s] + col_ref[c]
            at = pl.ds(pl.multiple_of(s * rows, rows), rows)
            c_all[c, at, :] = (total / denominator).astype(jnp.bfloat16)

        for p in (1, 2, 0):
            result(c, p).start()
        local_result(c).start()

    def compute_shed(h):
        p, u = order[h]

        @pl.loop(0, shed)
        def _(o):
            total = jnp.dot(a_shed[spot_of(p), piece(u), :], b_all[o], preferred_element_type=jnp.float32)
            denominator = row_ref[1, spot_of(p), piece(u), :] + col_ref[o]
            c_shed[o, at_rows(p, u), :] = (total / denominator).astype(jnp.bfloat16)
            back(o, h).start()

    lag = 2
    last = layers - 2

    for d in range(1, last):
        @pl.loop(0, chunks)
        def _(c):
            forward(d, c)

    @pl.when(is_end)
    def _():
        @pl.loop(0, chunks)
        def _(c):
            @pl.when(has_above)
            def _():
                along(c, layer, 1).wait_send()

            @pl.when(has_below)
            def _():
                along(c, layer, 0).wait_send()
        shed_z(0).start()

    @pl.loop(0, lag)
    def _(c):
        forward(last, c)

    local_a().wait()
    quad_a(1).wait_recv()
    quad_a(2).start()

    @pl.when(is_end)
    def _():
        shed_z(0).wait_send()
        shed_z(1).start()

    quad_a(0).wait_recv()
    quad_a(2).wait_recv()

    @pl.loop(lag, chunks + lag)
    def _(c):
        @pl.when(c < chunks)
        def _():
            forward(last, c)

        @pl.when(is_end & (c == chunks + lag - 1))
        def _():
            shed_z(1).wait_send()
            shed_z(2).start()

        @pl.when(is_helper & (c == lag + 1))
        def _():
            shed_z(0).wait_recv()
            shed_quad(0).start()
            shed_quad(1).start()

        @pl.when(due(c - lag))
        def _():
            compute(c - lag)

    @pl.when(is_helper)
    def _():
        shed_quad(1).wait_recv()
        compute_shed(0)
        compute_shed(1)
        shed_z(1).wait_recv()
        shed_quad(2).start()
        compute_shed(2)
        shed_quad(2).wait_recv()
        compute_shed(3)
        shed_quad(0).wait_recv()
        shed_quad(3).start()
        compute_shed(4)
        shed_quad(3).wait_recv()
        compute_shed(5)
        shed_z(2).wait_recv()
        shed_quad(4).start()
        compute_shed(6)
        shed_quad(4).wait_recv()
        compute_shed(7)
        for k in range(5):
            shed_quad(k).wait_send()
        for h in range(8):
            @pl.loop(0, shed)
            def _(o):
                back(o, h).wait_send()

    @pl.when(is_end)
    def _():
        for h in range(8):
            @pl.loop(0, shed)
            def _(o):
                back(o, h).wait_recv()
                deal(o, h).start()
        shed_z(2).wait_send()
        for h in range(8):
            @pl.loop(0, shed)
            def _(o):
                deal(o, h).wait()

    for p in range(3):
        quad_a(p).wait_send()

    @pl.loop(0, chunks)
    def _(c):
        for p in range(3):
            quad_b(c, p).wait_send()

        @pl.when(due(c))
        def _():
            local_result(c).wait()
            for p in range(3):
                result(c, p).wait()

        @pl.loop(0, layers)
        def _(owner):
            @pl.when((owner <= layer) & goes_up(c) & jnp.logical_not(is_end))
            def _():
                along(c, owner, 1).wait_send()

            @pl.when((owner >= layer) & goes_down(c) & jnp.logical_not(is_end))
            def _():
                along(c, owner, 0).wait_send()


def shards(amplitudes, integrals, occupied_energy, virtual_energy, pair_irrep):
    devices = lax.axis_size("row")
    layers = devices // QUAD
    rows, columns = amplitudes.shape
    depth = integrals.shape[0] * devices
    quarter = columns // QUAD
    width = 256
    chunks = quarter // width
    shed = chunks // 3
    position = lax.axis_index("row")
    pair_energy = pair_energies(occupied_energy, virtual_energy, pair_irrep)
    layer = position // QUAD
    upper = layer * 2 // layers
    depth_in = layer + upper * (layers - 1 - 2 * layer)
    mate = layer + (1 - 2 * upper) * (1 - 2 * depth_in)
    row_energy = jnp.stack([
        lax.dynamic_slice_in_dim(pair_energy, at * QUAD * rows, QUAD * rows) for at in (layer, mate)])
    col_energy = lax.dynamic_slice_in_dim(pair_energy, position % QUAD * quarter, quarter)
    dma = pltpu.SemaphoreType.DMA
    return pl.pallas_call(
        functools.partial(kernel, layers, chunks, shed),
        out_shape=jax.ShapeDtypeStruct((rows, columns), jnp.bfloat16),
        in_specs=[pl.BlockSpec(memory_space=pl.ANY)] * 2 + [pl.BlockSpec(memory_space=pltpu.VMEM)] * 2,
        out_specs=pl.BlockSpec(memory_space=pl.ANY),
        scratch_shapes=[
            pltpu.VMEM((QUAD, rows, depth), jnp.bfloat16),
            pltpu.VMEM((chunks, depth, width), jnp.bfloat16),
            pltpu.VMEM((chunks, QUAD * rows, width), jnp.bfloat16),
            pltpu.VMEM((QUAD, rows, depth), jnp.bfloat16),
            pltpu.VMEM((shed, QUAD * rows, width), jnp.bfloat16),
            dma((1 + chunks,)),
            dma((chunks, 3)),
            dma((chunks, 3)),
            dma((3,)),
            dma((3,)),
            dma((2, chunks, layers)),
            dma((chunks, layers)),
            dma((chunks, 3)),
            dma((chunks, 3)),
            dma((chunks,)),
            dma((3,)),
            dma((3,)),
            dma((5,)),
            dma((5,)),
            dma((shed, 8)),
            dma((shed, 8)),
            dma((shed, 2, 3)),
            dma((shed, 2, 3)),
            dma((shed, 2)),
        ],
        compiler_params=pltpu.CompilerParams(
            collective_id=0, has_side_effects=True, vmem_limit_bytes=63 * 1024 * 1024),
        cost_estimate=pl.CostEstimate(
            flops=2 * rows * depth * columns, bytes_accessed=6 * rows * columns, transcendentals=0),
    )(amplitudes, integrals, row_energy.reshape(2, QUAD, rows, 1), col_energy.reshape(chunks, 1, width))


def solution(mesh):
    in_specs = (P(("grp", "row"), None), P(("grp", "row"), None), P(), P(), P("grp"))
    out_specs = P(("grp", "row"), None)
    return jax.shard_map(shards, mesh=mesh, in_specs=in_specs, out_specs=out_specs, check_vma=False)
```

```python
import functools
import jax
import jax.numpy as jnp
from jax import lax
from jax.experimental import pallas as pl
from jax.experimental.pallas import tpu as pltpu
from jax.sharding import PartitionSpec as P

QUAD = 4
MESH = pl.DeviceIdType.MESH
UPPER, LOWER, LOWER_A, LOWER_B = (3, 3), (0, 3), (0, 2), (2, 1)
ORDER = ((3, UPPER), (0, UPPER), (3, LOWER), (0, LOWER), (1, UPPER), (2, UPPER),
         (1, LOWER_A), (2, LOWER_A), (1, LOWER_B), (2, LOWER_B))


def kernel(layers, chunks, shed, a_ref, b_ref, occupied_ref, virtual_ref, irrep_ref, out_ref, a_all,
           b_all, c_all, a_shed, c_shed, row_ref, col_ref, local_sem, bq_send, bq_recv, a_send, a_recv, z_send, z_recv, c_send, c_recv,
           c_local, az_send, az_recv, as_send, as_recv, cz_send, cz_recv, d_send, d_recv):
    rows = a_ref.shape[0]
    part = rows // 6
    width = b_all.shape[2]
    quarter = chunks * width
    layer_rows = QUAD * rows
    me = lax.axis_index("row")
    layer, spot = me // QUAD, me % QUAD
    half, core = spot // 2, spot % 2
    spots = ((half * 2) + (1 - core), (1 - half) * 2 + core, (1 - half) * 2 + (1 - core))
    peers = [layer * QUAD + s for s in spots]
    has_below, has_above = layer > 0, layer < layers - 1
    is_end = (layer == 0) | (layer == layers - 1)
    is_helper = (layer == 1) | (layer == layers - 2)
    upper = layer * 2 // layers
    depth = layer + upper * (layers - 1 - 2 * layer)
    mate = me + QUAD * (1 - 2 * upper) * (1 - 2 * depth)

    def local_a():
        return pltpu.make_async_copy(a_ref, a_all.at[spot], local_sem.at[0])

    def cols(owner, c):
        return pl.ds(pl.multiple_of(owner * quarter + c * width, width), width)

    def remote(src, dst, send, recv, device):
        return pltpu.make_async_remote_copy(
            src_ref=src, dst_ref=dst, send_sem=send, recv_sem=recv,
            device_id={"row": device}, device_id_type=MESH)

    def local_b(c):
        return pltpu.make_async_copy(
            b_ref.at[:, cols(spot, c)], b_all.at[c, pl.ds(me * rows, rows), :], local_sem.at[1 + c])

    def quad_b(c, p):
        return remote(b_ref.at[:, cols(spots[p], c)], b_all.at[c, pl.ds(me * rows, rows), :],
                      bq_send.at[c, p], bq_recv.at[c, p], peers[p])

    def quad_a(p):
        if p == 2:
            return remote(a_all.at[spots[1]], a_all.at[spots[1]], a_send.at[p], a_recv.at[p], peers[0])
        return remote(a_ref, a_all.at[spot], a_send.at[p], a_recv.at[p], peers[p])

    def along(c, owner, up):
        block = b_all.at[c, pl.ds(owner * layer_rows, layer_rows), :]
        return remote(block, block, z_send.at[up, c, owner], z_recv.at[c, owner],
                      me + QUAD if up else me - QUAD)

    def result(c, p):
        return remote(c_all.at[c, pl.ds(spots[p] * rows, rows), :], out_ref.at[:, cols(spot, c)],
                      c_send.at[c, p], c_recv.at[c, p], peers[p])

    def local_result(c):
        return pltpu.make_async_copy(
            c_all.at[c, pl.ds(spot * rows, rows), :], out_ref.at[:, cols(spot, c)], c_local.at[c])

    def piece(u):
        return pl.ds(u[0] * part, u[1] * part)

    def shed_z(k):
        u = (UPPER, LOWER, LOWER_A, LOWER_B)[k]
        src = a_all.at[spots[1], piece(u), :] if k > 1 else a_ref.at[piece(u), :]
        return remote(src, a_shed.at[spots[1] if k > 1 else spot, piece(u), :],
                      az_send.at[k], az_recv.at[k], mate)

    def shed_quad(k):
        u = (UPPER, UPPER, LOWER, UPPER, LOWER_A, LOWER_B)[k]
        at = a_shed.at[spot if k < 3 else spots[1], piece(u), :]
        return remote(at, at, as_send.at[k], as_recv.at[k], peers[1] if k == 0 else peers[0])

    def spot_of(p):
        return spot if p == 3 else spots[p]

    def at_rows(p, u):
        return pl.ds(spot_of(p) * rows + u[0] * part, u[1] * part)

    def back(o, h):
        at = at_rows(*ORDER[h])
        return remote(c_shed.at[o, at, :], c_all.at[o, at, :], cz_send.at[o, h], cz_recv.at[o, h], mate)

    def deal(o, h):
        p, u = ORDER[h]
        src, dst = c_all.at[o, at_rows(p, u), :], out_ref.at[piece(u), cols(spot, o)]
        if p == 3:
            return pltpu.make_async_copy(src, dst, d_send.at[o, h])
        return remote(src, dst, d_send.at[o, h], d_recv.at[o, h], peers[p])

    barrier = pltpu.get_barrier_semaphore()
    for p in range(3):
        pl.semaphore_signal(barrier, inc=1, device_id={"row": peers[p]}, device_id_type=MESH)

    @pl.when(has_below)
    def _():
        pl.semaphore_signal(barrier, inc=1, device_id={"row": me - QUAD}, device_id_type=MESH)

    @pl.when(has_above)
    def _():
        pl.semaphore_signal(barrier, inc=1, device_id={"row": me + QUAD}, device_id_type=MESH)

    pl.semaphore_wait(barrier, 3 + has_below.astype(jnp.int32) + has_above.astype(jnp.int32))

    @pl.loop(0, chunks)
    def _(c):
        local_b(c).start()
        for p in range(3):
            quad_b(c, p).start()

    @pl.when(is_end)
    def _():
        shed_z(0).start()

    local_a().start()
    quad_a(0).start()

    def goes_up(c):
        return has_above & ((layer < layers - 2) | (c >= shed))

    def goes_down(c):
        return has_below & ((layer > 1) | (c >= shed))

    def due(c):
        return jnp.logical_not(is_end) | (c >= shed)

    @pl.loop(0, chunks)
    def _(c):
        local_b(c).wait()
        for p in range(3):
            quad_b(c, p).wait_recv()

        @pl.when(goes_up(c))
        def _():
            along(c, layer, 1).start()

        @pl.when(goes_down(c))
        def _():
            along(c, layer, 0).start()

    quad_a(1).start()

    def forward(d, c):
        @pl.when((layer >= d) & goes_up(c))
        def _():
            along(c, layer - d, 1).wait_recv()
            along(c, layer - d, 1).start()

        @pl.when((layer + d < layers) & goes_down(c))
        def _():
            along(c, layer + d, 0).wait_recv()
            along(c, layer + d, 0).start()

    def compute(c):
        @pl.loop(0, layers)
        def _(owner):
            from_below, from_above = owner < layer, owner > layer
            passed_on = (from_below & goes_up(c)) | (from_above & goes_down(c))

            @pl.when((from_below | from_above) & jnp.logical_not(passed_on))
            def _():
                along(c, owner, 0).wait_recv()

        @pl.loop(0, QUAD)
        def _(s):
            total = jnp.dot(a_all[s], b_all[c], preferred_element_type=jnp.float32)
            at = pl.ds(pl.multiple_of(s * rows, rows), rows)
            denominator = row_ref[0, at, :] + col_ref[c]
            c_all[c, at, :] = (total / denominator).astype(jnp.bfloat16)

        for p in (1, 2, 0):
            result(c, p).start()
        local_result(c).start()

    def compute_shed(h):
        p, u = ORDER[h]

        @pl.loop(0, shed)
        def _(o):
            total = jnp.dot(a_shed[spot_of(p), piece(u), :], b_all[o], preferred_element_type=jnp.float32)
            denominator = row_ref[1, at_rows(p, u), :] + col_ref[o]
            c_shed[o, at_rows(p, u), :] = (total / denominator).astype(jnp.bfloat16)
            back(o, h).start()

    irreps, virtuals = virtual_ref.shape
    label = lax.broadcasted_iota(jnp.int32, (irreps, virtuals), 0)
    diagonal = (lax.broadcasted_iota(jnp.int32, (virtuals, virtuals), 0)
                == lax.broadcasted_iota(jnp.int32, (virtuals, virtuals), 1))

    def energies(orbital):
        chosen = jnp.where(label == irrep_ref[orbital], virtual_ref[...], 0.0)
        return jnp.sum(chosen, axis=0, keepdims=True) + occupied_ref[orbital]

    orbitals = layer_rows // virtuals
    for which, owner in enumerate((layer, layer + (1 - 2 * upper) * (1 - 2 * depth))):
        @pl.when((which == 0) | is_helper)
        def _():
            @pl.loop(0, orbitals)
            def _(i):
                along_lanes = jnp.broadcast_to(energies(owner * orbitals + i), (virtuals, virtuals))
                at = pl.ds(pl.multiple_of(i * virtuals, virtuals), virtuals)
                row_ref[which, at, :] = jnp.sum(jnp.where(diagonal, along_lanes, 0.0), axis=1, keepdims=True)

    per_chunk = width // virtuals

    @pl.loop(0, chunks)
    def _(c):
        for k in range(per_chunk):
            col_ref[c, :, k * virtuals:(k + 1) * virtuals] = energies(
                (spot * chunks + c) * per_chunk + k)

    lag = 2
    last = layers - 2

    for d in range(1, last):
        @pl.loop(0, chunks)
        def _(c):
            forward(d, c)

    @pl.when(is_end)
    def _():
        @pl.loop(0, chunks)
        def _(c):
            @pl.when(c == chunks - 1)
            def _():
                shed_z(1).start()

            @pl.when(has_above)
            def _():
                along(c, layer, 1).wait_send()

            @pl.when(has_below)
            def _():
                along(c, layer, 0).wait_send()

    @pl.loop(0, lag)
    def _(c):
        forward(last, c)

    local_a().wait()
    quad_a(1).wait_recv()
    quad_a(2).start()

    quad_a(0).wait_recv()
    quad_a(2).wait_recv()

    @pl.loop(lag, chunks + lag)
    def _(c):
        @pl.when(c < chunks)
        def _():
            forward(last, c)

        @pl.when(is_end & (c == chunks + lag - 2))
        def _():
            shed_z(2).start()
            shed_z(3).start()

        @pl.when(is_helper & (c == lag + 1))
        def _():
            shed_z(0).wait_recv()
            shed_quad(0).start()
            shed_quad(1).start()

        @pl.when(due(c - lag))
        def _():
            compute(c - lag)

    @pl.when(is_helper)
    def _():
        shed_quad(1).wait_recv()
        compute_shed(0)
        compute_shed(1)
        shed_z(1).wait_recv()
        shed_quad(2).start()
        compute_shed(2)
        shed_quad(2).wait_recv()
        compute_shed(3)
        shed_quad(0).wait_recv()
        shed_quad(3).start()
        compute_shed(4)
        shed_quad(3).wait_recv()
        compute_shed(5)
        for k in (2, 3):
            shed_z(k).wait_recv()
            shed_quad(k + 2).start()
            compute_shed(2 * k + 2)
            shed_quad(k + 2).wait_recv()
            compute_shed(2 * k + 3)
        for k in range(6):
            shed_quad(k).wait_send()
        for h in range(len(ORDER)):
            @pl.loop(0, shed)
            def _(o):
                back(o, h).wait_send()

    @pl.when(is_end)
    def _():
        for h in range(len(ORDER)):
            @pl.loop(0, shed)
            def _(o):
                back(o, h).wait_recv()
                deal(o, h).start()
        for k in range(4):
            shed_z(k).wait_send()
        for h in range(len(ORDER)):
            @pl.loop(0, shed)
            def _(o):
                deal(o, h).wait()

    for p in range(3):
        quad_a(p).wait_send()

    @pl.loop(0, chunks)
    def _(c):
        for p in range(3):
            quad_b(c, p).wait_send()

        @pl.when(due(c))
        def _():
            local_result(c).wait()
            for p in range(3):
                result(c, p).wait()

        @pl.loop(0, layers)
        def _(owner):
            @pl.when((owner <= layer) & goes_up(c) & jnp.logical_not(is_end))
            def _():
                along(c, owner, 1).wait_send()

            @pl.when((owner >= layer) & goes_down(c) & jnp.logical_not(is_end))
            def _():
                along(c, owner, 0).wait_send()


def shards(amplitudes, integrals, occupied_energy, virtual_energy, pair_irrep):
    devices = lax.axis_size("row")
    layers = devices // QUAD
    rows, columns = amplitudes.shape
    depth = integrals.shape[0] * devices
    quarter = columns // QUAD
    width = 256
    chunks = quarter // width
    shed = chunks // 3
    dma = pltpu.SemaphoreType.DMA
    return pl.pallas_call(
        functools.partial(kernel, layers, chunks, shed),
        out_shape=jax.ShapeDtypeStruct((rows, columns), jnp.bfloat16),
        in_specs=[pl.BlockSpec(memory_space=space) for space in (
            pl.ANY, pl.ANY, pltpu.SMEM, pltpu.VMEM, pltpu.SMEM)],
        out_specs=pl.BlockSpec(memory_space=pl.ANY),
        scratch_shapes=[
            pltpu.VMEM((QUAD, rows, depth), jnp.bfloat16),
            pltpu.VMEM((chunks, depth, width), jnp.bfloat16),
            pltpu.VMEM((chunks, QUAD * rows, width), jnp.bfloat16),
            pltpu.VMEM((QUAD, rows, depth), jnp.bfloat16),
            pltpu.VMEM((shed, QUAD * rows, width), jnp.bfloat16),
            pltpu.VMEM((2, QUAD * rows, 1), jnp.float32),
            pltpu.VMEM((chunks, 1, width), jnp.float32),
            dma((1 + chunks,)),
            dma((chunks, 3)),
            dma((chunks, 3)),
            dma((3,)),
            dma((3,)),
            dma((2, chunks, layers)),
            dma((chunks, layers)),
            dma((chunks, 3)),
            dma((chunks, 3)),
            dma((chunks,)),
            dma((4,)),
            dma((4,)),
            dma((6,)),
            dma((6,)),
            dma((shed, len(ORDER))),
            dma((shed, len(ORDER))),
            dma((shed, len(ORDER))),
            dma((shed, len(ORDER))),
        ],
        compiler_params=pltpu.CompilerParams(
            collective_id=0, has_side_effects=True, vmem_limit_bytes=63 * 1024 * 1024),
        cost_estimate=pl.CostEstimate(
            flops=2 * rows * depth * columns, bytes_accessed=6 * rows * columns, transcendentals=0),
    )(amplitudes, integrals, occupied_energy, virtual_energy, pair_irrep)


def solution(mesh):
    in_specs = (P(("grp", "row"), None), P(("grp", "row"), None), P(), P(), P("grp"))
    out_specs = P(("grp", "row"), None)
    return jax.shard_map(shards, mesh=mesh, in_specs=in_specs, out_specs=out_specs, check_vma=False)
```

```python
import functools
import jax
import jax.numpy as jnp
from jax import lax
from jax.experimental import pallas as pl
from jax.experimental.pallas import tpu as pltpu
from jax.sharding import PartitionSpec as P

QUAD = 4
MESH = pl.DeviceIdType.MESH
UPPER, LOWER, LOWER_A, LOWER_B = (3, 3), (0, 3), (0, 2), (2, 1)
ORDER = ((3, UPPER), (0, UPPER), (3, LOWER), (0, LOWER), (1, UPPER), (2, UPPER),
         (1, LOWER_A), (2, LOWER_A), (1, LOWER_B), (2, LOWER_B))


def kernel(layers, chunks, shed, a_ref, b_ref, occupied_ref, virtual_ref, irrep_ref, out_ref, a_all,
           b_all, c_all, a_shed, c_shed, row_ref, col_ref, local_sem, bq_send, bq_recv, a_send, a_recv, z_send, z_recv, c_send, c_recv,
           c_local, az_send, az_recv, as_send, as_recv, cz_send, cz_recv, d_send, d_recv):
    rows = a_ref.shape[0]
    part = rows // 6
    width = b_all.shape[2]
    quarter = chunks * width
    layer_rows = QUAD * rows
    me = lax.axis_index("row")
    layer, spot = me // QUAD, me % QUAD
    half, core = spot // 2, spot % 2
    spots = ((half * 2) + (1 - core), (1 - half) * 2 + core, (1 - half) * 2 + (1 - core))
    peers = [layer * QUAD + s for s in spots]
    has_below, has_above = layer > 0, layer < layers - 1
    is_end = (layer == 0) | (layer == layers - 1)
    is_helper = (layer == 1) | (layer == layers - 2)
    upper = layer * 2 // layers
    depth = layer + upper * (layers - 1 - 2 * layer)
    mate = me + QUAD * (1 - 2 * upper) * (1 - 2 * depth)

    def local_a():
        return pltpu.make_async_copy(a_ref, a_all.at[spot], local_sem.at[0])

    def cols(owner, c):
        return pl.ds(pl.multiple_of(owner * quarter + c * width, width), width)

    def remote(src, dst, send, recv, device):
        return pltpu.make_async_remote_copy(
            src_ref=src, dst_ref=dst, send_sem=send, recv_sem=recv,
            device_id={"row": device}, device_id_type=MESH)

    def local_b(c):
        return pltpu.make_async_copy(
            b_ref.at[:, cols(spot, c)], b_all.at[c, pl.ds(me * rows, rows), :], local_sem.at[1 + c])

    def quad_b(c, p):
        return remote(b_ref.at[:, cols(spots[p], c)], b_all.at[c, pl.ds(me * rows, rows), :],
                      bq_send.at[c, p], bq_recv.at[c, p], peers[p])

    def quad_a(p):
        if p == 2:
            return remote(a_all.at[spots[1]], a_all.at[spots[1]], a_send.at[p], a_recv.at[p], peers[0])
        return remote(a_ref, a_all.at[spot], a_send.at[p], a_recv.at[p], peers[p])

    def along(c, owner, up):
        block = b_all.at[c, pl.ds(owner * layer_rows, layer_rows), :]
        return remote(block, block, z_send.at[up, c, owner], z_recv.at[c, owner],
                      me + QUAD if up else me - QUAD)

    def result(c, p):
        return remote(c_all.at[c, pl.ds(spots[p] * rows, rows), :], out_ref.at[:, cols(spot, c)],
                      c_send.at[c, p], c_recv.at[c, p], peers[p])

    def local_result(c):
        return pltpu.make_async_copy(
            c_all.at[c, pl.ds(spot * rows, rows), :], out_ref.at[:, cols(spot, c)], c_local.at[c])

    def piece(u):
        return pl.ds(u[0] * part, u[1] * part)

    def shed_z(k):
        u = (UPPER, LOWER, LOWER_A, LOWER_B)[k]
        src = a_all.at[spots[1], piece(u), :] if k > 1 else a_ref.at[piece(u), :]
        return remote(src, a_shed.at[spots[1] if k > 1 else spot, piece(u), :],
                      az_send.at[k], az_recv.at[k], mate)

    def shed_quad(k):
        u = (UPPER, UPPER, LOWER, UPPER, LOWER_A, LOWER_B)[k]
        at = a_shed.at[spot if k < 3 else spots[1], piece(u), :]
        return remote(at, at, as_send.at[k], as_recv.at[k], peers[1] if k == 0 else peers[0])

    def spot_of(p):
        return spot if p == 3 else spots[p]

    def at_rows(p, u):
        return pl.ds(spot_of(p) * rows + u[0] * part, u[1] * part)

    def back(o, h):
        at = at_rows(*ORDER[h])
        return remote(c_shed.at[o, at, :], c_all.at[o, at, :], cz_send.at[o, h], cz_recv.at[o, h], mate)

    def deal(o, h):
        p, u = ORDER[h]
        src, dst = c_all.at[o, at_rows(p, u), :], out_ref.at[piece(u), cols(spot, o)]
        if p == 3:
            return pltpu.make_async_copy(src, dst, d_send.at[o, h])
        return remote(src, dst, d_send.at[o, h], d_recv.at[o, h], peers[p])

    barrier = pltpu.get_barrier_semaphore()
    for p in range(3):
        pl.semaphore_signal(barrier, inc=1, device_id={"row": peers[p]}, device_id_type=MESH)

    @pl.when(has_below)
    def _():
        pl.semaphore_signal(barrier, inc=1, device_id={"row": me - QUAD}, device_id_type=MESH)

    @pl.when(has_above)
    def _():
        pl.semaphore_signal(barrier, inc=1, device_id={"row": me + QUAD}, device_id_type=MESH)

    pl.semaphore_wait(barrier, 3 + has_below.astype(jnp.int32) + has_above.astype(jnp.int32))

    @pl.loop(0, chunks)
    def _(c):
        local_b(c).start()
        for p in range(3):
            quad_b(c, p).start()

    @pl.when(is_end)
    def _():
        shed_z(0).start()

    local_a().start()
    quad_a(0).start()

    def goes_up(c):
        return has_above & ((layer < layers - 2) | (c >= shed))

    def goes_down(c):
        return has_below & ((layer > 1) | (c >= shed))

    def due(c):
        return jnp.logical_not(is_end) | (c >= shed)

    @pl.loop(0, chunks)
    def _(c):
        local_b(c).wait()
        for p in range(3):
            quad_b(c, p).wait_recv()

        @pl.when(goes_up(c))
        def _():
            along(c, layer, 1).start()

        @pl.when(goes_down(c))
        def _():
            along(c, layer, 0).start()

    quad_a(1).start()

    def forward(d, c):
        @pl.when((layer >= d) & goes_up(c))
        def _():
            along(c, layer - d, 1).wait_recv()
            along(c, layer - d, 1).start()

        @pl.when((layer + d < layers) & goes_down(c))
        def _():
            along(c, layer + d, 0).wait_recv()
            along(c, layer + d, 0).start()

    held = min(2, chunks - 1)

    def send(c):
        for p in (1, 2, 0):
            result(c, p).start()
        local_result(c).start()

    def compute(c):
        @pl.loop(0, layers)
        def _(owner):
            from_below, from_above = owner < layer, owner > layer
            passed_on = (from_below & goes_up(c)) | (from_above & goes_down(c))

            @pl.when((from_below | from_above) & jnp.logical_not(passed_on))
            def _():
                along(c, owner, 0).wait_recv()

        @pl.loop(0, QUAD)
        def _(s):
            total = jnp.dot(a_all[s], b_all[c], preferred_element_type=jnp.float32)
            at = pl.ds(pl.multiple_of(s * rows, rows), rows)
            denominator = row_ref[0, at, :] + col_ref[c]
            c_all[c, at, :] = (total / denominator).astype(jnp.bfloat16)

        @pl.when(jnp.logical_not(is_helper) | (c > held))
        def _():
            send(c)

        @pl.when(is_helper & (c == held))
        def _():
            shed_quad(0).wait_send()

            @pl.loop(0, held + 1)
            def _(k):
                send(k)

    def compute_shed(h):
        p, u = ORDER[h]

        @pl.loop(0, shed)
        def _(o):
            total = jnp.dot(a_shed[spot_of(p), piece(u), :], b_all[o], preferred_element_type=jnp.float32)
            denominator = row_ref[1, at_rows(p, u), :] + col_ref[o]
            c_shed[o, at_rows(p, u), :] = (total / denominator).astype(jnp.bfloat16)
            back(o, h).start()

    irreps, virtuals = virtual_ref.shape
    label = lax.broadcasted_iota(jnp.int32, (irreps, virtuals), 0)
    diagonal = (lax.broadcasted_iota(jnp.int32, (virtuals, virtuals), 0)
                == lax.broadcasted_iota(jnp.int32, (virtuals, virtuals), 1))

    def energies(orbital):
        chosen = jnp.where(label == irrep_ref[orbital], virtual_ref[...], 0.0)
        return jnp.sum(chosen, axis=0, keepdims=True) + occupied_ref[orbital]

    orbitals = layer_rows // virtuals
    for which, owner in enumerate((layer, layer + (1 - 2 * upper) * (1 - 2 * depth))):
        @pl.when((which == 0) | is_helper)
        def _():
            @pl.loop(0, orbitals)
            def _(i):
                along_lanes = jnp.broadcast_to(energies(owner * orbitals + i), (virtuals, virtuals))
                at = pl.ds(pl.multiple_of(i * virtuals, virtuals), virtuals)
                row_ref[which, at, :] = jnp.sum(jnp.where(diagonal, along_lanes, 0.0), axis=1, keepdims=True)

    per_chunk = width // virtuals

    @pl.loop(0, chunks)
    def _(c):
        for k in range(per_chunk):
            col_ref[c, :, k * virtuals:(k + 1) * virtuals] = energies(
                (spot * chunks + c) * per_chunk + k)

    lag = 2
    last = layers - 2

    for d in range(1, last):
        @pl.loop(0, chunks)
        def _(c):
            forward(d, c)

    @pl.when(is_end)
    def _():
        @pl.loop(0, chunks)
        def _(c):
            @pl.when(c == chunks - 1)
            def _():
                shed_z(1).start()

            @pl.when(has_above)
            def _():
                along(c, layer, 1).wait_send()

            @pl.when(has_below)
            def _():
                along(c, layer, 0).wait_send()

    @pl.loop(0, lag)
    def _(c):
        forward(last, c)

    local_a().wait()
    quad_a(1).wait_recv()
    quad_a(2).start()

    @pl.when(is_helper)
    def _():
        shed_z(0).wait_recv()
        shed_quad(0).start()
        shed_quad(1).start()

    quad_a(0).wait_recv()
    quad_a(2).wait_recv()

    @pl.loop(lag, chunks + lag)
    def _(c):
        @pl.when(c < chunks)
        def _():
            forward(last, c)

        @pl.when(is_end & (c == chunks + lag - 2))
        def _():
            shed_z(2).start()
            shed_z(3).start()

        @pl.when(due(c - lag))
        def _():
            compute(c - lag)

    @pl.when(is_helper)
    def _():
        shed_quad(1).wait_recv()
        compute_shed(0)
        compute_shed(1)
        shed_z(1).wait_recv()
        shed_quad(2).start()
        compute_shed(2)
        shed_quad(2).wait_recv()
        compute_shed(3)
        shed_quad(0).wait_recv()
        shed_quad(3).start()
        compute_shed(4)
        shed_quad(3).wait_recv()
        compute_shed(5)
        for k in (2, 3):
            shed_z(k).wait_recv()
            shed_quad(k + 2).start()
            compute_shed(2 * k + 2)
            shed_quad(k + 2).wait_recv()
            compute_shed(2 * k + 3)
        for k in range(1, 6):
            shed_quad(k).wait_send()
        for h in range(len(ORDER)):
            @pl.loop(0, shed)
            def _(o):
                back(o, h).wait_send()

    @pl.when(is_end)
    def _():
        for h in range(len(ORDER)):
            @pl.loop(0, shed)
            def _(o):
                back(o, h).wait_recv()
                deal(o, h).start()
        for k in range(4):
            shed_z(k).wait_send()
        for h in range(len(ORDER)):
            @pl.loop(0, shed)
            def _(o):
                deal(o, h).wait()

    for p in range(3):
        quad_a(p).wait_send()

    @pl.loop(0, chunks)
    def _(c):
        for p in range(3):
            quad_b(c, p).wait_send()

        @pl.when(due(c))
        def _():
            local_result(c).wait()
            for p in range(3):
                result(c, p).wait()

        @pl.loop(0, layers)
        def _(owner):
            @pl.when((owner <= layer) & goes_up(c) & jnp.logical_not(is_end))
            def _():
                along(c, owner, 1).wait_send()

            @pl.when((owner >= layer) & goes_down(c) & jnp.logical_not(is_end))
            def _():
                along(c, owner, 0).wait_send()


def shards(amplitudes, integrals, occupied_energy, virtual_energy, pair_irrep):
    devices = lax.axis_size("row")
    layers = devices // QUAD
    rows, columns = amplitudes.shape
    depth = integrals.shape[0] * devices
    quarter = columns // QUAD
    width = 256
    chunks = quarter // width
    shed = chunks // 3
    dma = pltpu.SemaphoreType.DMA
    return pl.pallas_call(
        functools.partial(kernel, layers, chunks, shed),
        out_shape=jax.ShapeDtypeStruct((rows, columns), jnp.bfloat16),
        in_specs=[pl.BlockSpec(memory_space=space) for space in (
            pl.ANY, pl.ANY, pltpu.SMEM, pltpu.VMEM, pltpu.SMEM)],
        out_specs=pl.BlockSpec(memory_space=pl.ANY),
        scratch_shapes=[
            pltpu.VMEM((QUAD, rows, depth), jnp.bfloat16),
            pltpu.VMEM((chunks, depth, width), jnp.bfloat16),
            pltpu.VMEM((chunks, QUAD * rows, width), jnp.bfloat16),
            pltpu.VMEM((QUAD, rows, depth), jnp.bfloat16),
            pltpu.VMEM((shed, QUAD * rows, width), jnp.bfloat16),
            pltpu.VMEM((2, QUAD * rows, 1), jnp.float32),
            pltpu.VMEM((chunks, 1, width), jnp.float32),
            dma((1 + chunks,)),
            dma((chunks, 3)),
            dma((chunks, 3)),
            dma((3,)),
            dma((3,)),
            dma((2, chunks, layers)),
            dma((chunks, layers)),
            dma((chunks, 3)),
            dma((chunks, 3)),
            dma((chunks,)),
            dma((4,)),
            dma((4,)),
            dma((6,)),
            dma((6,)),
            dma((shed, len(ORDER))),
            dma((shed, len(ORDER))),
            dma((shed, len(ORDER))),
            dma((shed, len(ORDER))),
        ],
        compiler_params=pltpu.CompilerParams(
            collective_id=0, has_side_effects=True, vmem_limit_bytes=63 * 1024 * 1024),
        cost_estimate=pl.CostEstimate(
            flops=2 * rows * depth * columns, bytes_accessed=6 * rows * columns, transcendentals=0),
    )(amplitudes, integrals, occupied_energy, virtual_energy, pair_irrep)


def solution(mesh):
    in_specs = (P(("grp", "row"), None), P(("grp", "row"), None), P(), P(), P("grp"))
    out_specs = P(("grp", "row"), None)
    return jax.shard_map(shards, mesh=mesh, in_specs=in_specs, out_specs=out_specs, check_vma=False)
```
